32 devices in a mesh: region: 2 (over y), rows: 16 (over z, x, core).
Axes of the slice: x: 2, y: 2, z: 4, core: 2. Of those that a mesh axis runs over, the one named last changes fastest.
Arguments:
- features: bfloat16 [20480, 768], P(('region', 'rows')), parts along dimension 0
- seed_labels: int32 [20480], P(('region', 'rows')), parts along dimension 0, may hold values from -1 to 1023, as said below
- neighbours: int32 [160, 16], P(('region', 'rows')), parts along dimension 0, may hold values from 0 to 79, as said below
- hub_blocks: int32 [8], P('region'), parts along dimension 0, may hold values from 0 to 79, as said below
Outputs:
- scores: float32 [20480, 1024], P(('region', 'rows')), parts along dimension 0
The draws below stay inside these ranges and needn't reach their ends.
There are 2 independent parts, one for each index of `region`. The reference program is written for one: setup_inputs(seed, part) draws one part's arguments, and reference() takes and returns one part's arrays. A program takes and returns all parts, laid end to end along the dimension named above; each array names one. Nothing has to cross between parts.
Inputs may be any that keep to these rules, and one draw needn't show every extreme that they name: `seed_labels`: each block of 128 crops holds at least two labelled crops. `neighbours`: slot 0 of block b is b itself; the other slots name distinct blocks at most 10 blocks away from b along the closed loop of the 80 blocks (b - 1 and b + 1 beside it, 0 beside 80 - 1). `hub_blocks`: the hub ids are distinct, and one of them is 79.
All inputs are finite; a program needn't handle non-finite values.
Results may differ from the reference program's by a relative error of at most 0.00095.
Values may be sent and summed in bfloat16 or wider, within the bound.
A program may use at most 128 MiB of HBM per device.

```python
import jax
import jax.numpy as jnp
from jax import lax

BLK = 128
BLK_DEV = 5
K = 16
HUBS = 4
C = 1024
D = 768
ITERS = 3
NB = 80
ROWS = 10240


def draw_hub_blocks(key, part):
    key = jax.random.fold_in(key, 13)
    first, second = jax.random.split(key, 2)
    others = jax.random.permutation(first, NB - 1)[:HUBS - 1].astype(jnp.int32)
    joined = jnp.concatenate([others, jnp.full((1,), NB - 1, jnp.int32)], axis=0)
    order = jax.random.permutation(second, HUBS)
    return joined[order].astype(jnp.int32)


def draw_neighbours(key, part):
    key = jax.random.fold_in(key, 11)
    blocks = jnp.arange(NB, dtype=jnp.int32)
    distance = (blocks[None, :] - blocks[:, None]) % NB
    beside_all = jnp.minimum(distance, NB - distance)
    near_block = beside_all <= 2 * BLK_DEV
    base = jax.random.randint(key, (NB, NB), 0, 1024, dtype=jnp.int32)
    score = base * 2048 + blocks[None, :]
    score = score + jnp.where(distance == 0, 1 << 23, 0)
    score = jnp.where(near_block, score, -1)
    picked = lax.top_k(score, K)[1]
    return picked.astype(jnp.int32)


def draw_features(key, part):
    key = jax.random.fold_in(key, 5)
    first, second, third = jax.random.split(key, 3)
    groups = jax.random.randint(first, (ROWS,), 0, 16, dtype=jnp.int32)
    centres = jax.random.normal(second, (16, D), jnp.float32)
    noise = jax.random.normal(third, (ROWS, D), jnp.float32)
    values = noise + 1.5 * centres[groups]
    return values.astype(jnp.bfloat16)


def draw_seed_labels(key, part):
    key = jax.random.fold_in(key, 7)
    first, second, third = jax.random.split(key, 3)
    labelled = jax.random.randint(first, (ROWS,), 0, 10, dtype=jnp.int32) < 3
    chosen = jax.random.randint(second, (NB,), 0, BLK, dtype=jnp.int32)
    position = jnp.arange(ROWS, dtype=jnp.int32) % BLK
    owner = jnp.arange(ROWS, dtype=jnp.int32) // BLK
    forced = (position == chosen[owner]) | (position == (chosen[owner] + BLK // 2) % BLK)
    taxa = jax.random.randint(third, (ROWS,), 0, C, dtype=jnp.int32)
    return jnp.where(labelled | forced, taxa, -1).astype(jnp.int32)


def setup_inputs(seed: int = 0, part: int = 0) -> dict:
    key_of = jax.random.split(jax.random.key(seed), 5)
    part_splits = jax.random.split(jax.random.fold_in(key_of[4], part), 5)
    return {
        "features": draw_features(jax.random.fold_in(jax.random.fold_in(key_of[4], part), 71), part),
        "seed_labels": draw_seed_labels(jax.random.fold_in(jax.random.fold_in(key_of[4], part), 71), part),
        "neighbours": draw_neighbours(jax.random.fold_in(jax.random.fold_in(key_of[4], part), 71), part),
        "hub_blocks": draw_hub_blocks(jax.random.fold_in(jax.random.fold_in(key_of[4], part), 71), part),
    }


spread_rate = 0.9
kernel_width = 0.25
epsilon = 1e-06

def unit_rows(features):
    values = features.astype(jnp.float32)
    scaled = values * lax.rsqrt(lax.optimization_barrier(jnp.mean(values * values, axis=1, keepdims=True)) + epsilon)
    return (scaled * features.shape[1] ** (-0.5)).astype(jnp.bfloat16)

def block_kernel(own_rows, gathered, neighbour_row, block_id):
    count, rows_per, width = gathered.shape
    flat = gathered.reshape(count * rows_per, width)
    dots = jnp.dot(own_rows, flat.T, preferred_element_type=jnp.float32)
    kernel = jnp.exp((dots - 1.0) / kernel_width)
    line = jnp.arange(rows_per, dtype=jnp.int32)
    diagonal_mask = line[:, None, None] == line[None, None, :]
    self_slot = (neighbour_row == block_id)[None, :, None]
    same_crop = (diagonal_mask & self_slot).reshape(rows_per, count * rows_per)
    kernel = jnp.where(same_crop, jnp.float32(0.0), kernel)
    degree = lax.optimization_barrier(jnp.sum(kernel, axis=1))
    return (kernel.astype(jnp.bfloat16), degree)

def reference(features, seed_labels, neighbours, hub_blocks):
    unit = unit_rows(features).reshape(NB, BLK, D)
    block_ids = jnp.arange(NB, dtype=jnp.int32)
    listed = jnp.concatenate([neighbours.astype(jnp.int32), jnp.broadcast_to(hub_blocks.astype(jnp.int32)[None, :], (NB, HUBS))], axis=1)

    def weigh(packed):
        own_rows, neighbour_row, block_id = packed
        return block_kernel(own_rows, unit[neighbour_row], neighbour_row, block_id)
    weights, degree = lax.map(weigh, (unit, listed, block_ids))
    inverse_root = lax.rsqrt(degree).reshape(ROWS, 1)
    seeds = (seed_labels[:, None] == jnp.arange(C, dtype=jnp.int32)[None, :]).astype(jnp.float32)
    spread = seeds
    for iteration in range(ITERS):
        scaled = (inverse_root * spread).astype(jnp.bfloat16).reshape(NB, BLK, C)

        def apply(packed):
            block_weights, neighbour_row = packed
            gathered = scaled[neighbour_row].reshape((K + HUBS) * BLK, C)
            return jnp.dot(block_weights, gathered, preferred_element_type=jnp.float32)
        gathered_sum = lax.map(apply, (weights, listed)).reshape(ROWS, C)
        spread = spread_rate * inverse_root * gathered_sum + (1.0 - spread_rate) * seeds
    totals = lax.optimization_barrier(jnp.sum(spread, axis=1, keepdims=True))
    return jnp.log(1.0 + C * spread / totals)
```

```python
import functools
import math

import jax
import jax.numpy as jnp
from jax import lax
from jax.experimental import pallas as pl
from jax.experimental.pallas import tpu as pltpu
from jax.sharding import PartitionSpec as P

ITERS = 3
GROUP = 4
LOG2E = math.log2(math.e)

spread_rate = 0.9
kernel_width = 0.25
epsilon = 1e-06


def kernel(groups, blk, cols, feat_ref, meta_ref, hub_ref, out_ref,
           table, weights, labels, inv_root, label_col, meta, bias,
           hub_send, hub_recv, lab_send, lab_recv, res, res_half, from_sib, from_x, from_d, pick,
           f_send, f_recv, m_send, m_recv, h_send, h_recv, p_send, p_recv,
           z_send, z_recv, l_send, l_recv, r_send, r_recv):
    own_blocks = feat_ref.shape[0] // blk
    width = feat_ref.shape[1]
    reach = 2 * own_blocks
    group_blocks = GROUP * own_blocks
    window = group_blocks + 2 * reach
    hubs = GROUP
    pairs = group_blocks // 2
    span = (2 * reach + 2) * blk
    quarter = cols // GROUP
    stages = groups.bit_length() - 1

    me = lax.axis_index("rows")
    g, q = lax.div(me, GROUP), lax.rem(me, GROUP)
    c, x = lax.rem(q, 2), lax.div(q, 2)
    q_sib = q + 1 - 2 * c
    q_x = q + 2 - 4 * x
    q_d = q_x + 1 - 2 * c
    sib, xp, dp = g * GROUP + q_sib, g * GROUP + q_x, g * GROUP + q_d
    up = lax.rem(g + 1, groups) * GROUP + q
    down = lax.rem(g + groups - 1, groups) * GROUP + q
    first = x * up + (1 - x) * down
    second = x * down + (1 - x) * up
    partners = []
    for s in range(stages):
        size = 2 ** (s + 1)
        pg = lax.div(g, size) * size + size - 1 - lax.rem(g, size)
        partners.append(pg * GROUP + q)

    def remote(src, dst, send, recv, device):
        return pltpu.make_async_remote_copy(
            src_ref=src, dst_ref=dst, send_sem=send, recv_sem=recv,
            device_id={"rows": device}, device_id_type=pl.DeviceIdType.MESH)

    barrier = pltpu.get_barrier_semaphore()
    everyone = [sib, xp, dp, up, down] + partners
    for device in everyone:
        pl.semaphore_signal(barrier, inc=1, device_id={"rows": device},
                            device_id_type=pl.DeviceIdType.MESH)
    pl.semaphore_wait(barrier, len(everyone))

    pending = []

    def at(position):
        return pl.ds(pl.multiple_of(position * blk, blk), blk)

    meta[q] = meta_ref[...]
    meta_copies = []
    for k, device in enumerate((sib, xp, dp)):
        copy = remote(meta.at[q], meta.at[q], m_send.at[k], m_recv.at[k], device)
        copy.start()
        meta_copies.append(copy)

    pos_a = reach + own_blocks * q
    pos_b = reach + own_blocks * q_x
    edge = reach + group_blocks
    dst_a = x * (own_blocks * c) + (1 - x) * (edge + own_blocks * c)
    dst_b = (1 - x) * (own_blocks * c) + x * (edge + own_blocks * c)

    def fcopy(kind, n, src, dst, device):
        return remote(table.at[at(src + n)], table.at[at(dst + n)],
                      f_send.at[kind, n], f_recv.at[kind, n], device)

    a_x, a_z, a_s, b_z, b_s, ha_s, hb_s = [], [], [], [], [], [], []
    for n in range(own_blocks):
        values = feat_ref[n * blk:(n + 1) * blk, :].astype(jnp.float32)
        mean = jnp.sum(values * values, axis=1, keepdims=True) * (1.0 / width)
        scaled = values * lax.rsqrt(mean + epsilon)
        table[at(pos_a + n), :] = (scaled * width ** (-0.5)).astype(jnp.bfloat16)
        a_x.append(fcopy(0, n, pos_a, pos_a, xp))
        a_z.append(fcopy(1, n, pos_a, dst_a, first))
        a_s.append(fcopy(2, n, pos_a, pos_a, sib))
        a_x[n].start()
        a_z[n].start()
        a_s[n].start()
    for n in range(own_blocks):
        a_x[n].wait_recv()
        b_z.append(fcopy(3, n, pos_b, dst_b, second))
        b_s.append(fcopy(4, n, pos_b, pos_b, sib))
        b_z[n].start()
        b_s[n].start()
    for n in range(own_blocks):
        a_s[n].wait_recv()
        b_s[n].wait_recv()

    base_block = g * group_blocks
    row = lax.broadcasted_iota(jnp.int32, (blk, blk), 0)
    col = lax.broadcasted_iota(jnp.int32, (blk, blk), 1)
    for h in range(hubs):
        for n in range(group_blocks):
            off = (hub_ref[h] - (base_block + n)) * 1024
            pick[h * blk:(h + 1) * blk, n * blk:(n + 1) * blk] = jnp.where(
                row - col + off == 0, 1.0, 0.0).astype(jnp.bfloat16)
    low, high = reach * blk, (reach + group_blocks) * blk
    held = jnp.dot(pick[at(q), :], table[low:high, :],
                   preferred_element_type=jnp.float32).astype(jnp.bfloat16)
    for s in range(stages):
        hub_send[s] = held
        copy = remote(hub_send.at[s], hub_recv.at[s], h_send.at[s], h_recv.at[s], partners[s])
        copy.start()
        pending.append(copy)
        copy.wait_recv()
        held = held + hub_recv[s]
    table[at(window + q), :] = held
    hub_copies = []
    for k, device in enumerate((sib, xp, dp)):
        copy = remote(table.at[at(window + q)], table.at[at(window + q)],
                      p_send.at[k], p_recv.at[k], device)
        copy.start()
        hub_copies.append(copy)

    for n in range(own_blocks):
        a_z[n].wait_recv()
        ha_s.append(fcopy(5, n, dst_a, dst_a, sib))
        ha_s[n].start()
    for n in range(own_blocks):
        b_z[n].wait_recv()
        hb_s.append(fcopy(6, n, dst_b, dst_b, sib))
        hb_s[n].start()

    for copy in meta_copies:
        copy.wait_recv()
    for n in range(group_blocks):
        owner, at_n = n // own_blocks, n % own_blocks
        bias[n:n + 1, :] = meta[owner, 8 + at_n:9 + at_n, :]
        line = jnp.broadcast_to(meta[owner, at_n:at_n + 1, :], (blk, blk))
        column = jnp.sum(jnp.where(row == col, line, 0.0), axis=1, keepdims=True)
        label_col[n * blk:(n + 1) * blk, :] = jnp.broadcast_to(column, (blk, blk)).astype(jnp.int32)

    for copy in ha_s + hb_s + hub_copies:
        copy.wait_recv()
    pending += meta_copies + a_x + a_z + a_s + b_z + b_s + ha_s + hb_s + hub_copies

    two = 2 * blk
    row2 = lax.broadcasted_iota(jnp.int32, (two, two), 0)
    col2 = lax.broadcasted_iota(jnp.int32, (two, two), 1)
    factor = LOG2E / kernel_width

    def weigh(m, carry):
        own = table[pl.ds(pl.multiple_of((reach + 2 * m) * blk, blk), two), :]
        lines = (bias[pl.ds(2 * m, 1), :], bias[pl.ds(2 * m + 1, 1), :])
        total = jnp.zeros((two, blk), jnp.float32)
        for k in range(reach + 1 + hubs // 2):
            if k <= reach:
                start = pl.multiple_of(2 * m * blk + k * two, blk)
            else:
                start = window * blk + (k - reach - 1) * two
            slab = table[pl.ds(start, two), :]
            dots = lax.dot_general(own, slab, (((1,), (1,)), ((), ())),
                                   preferred_element_type=jnp.float32)
            dots = dots * factor
            if k <= reach:
                parts = []
                for half in range(2):
                    line = jnp.concatenate(
                        [jnp.broadcast_to(lines[half][:, 2 * k + j:2 * k + j + 1], (1, blk))
                         for j in range(2)], axis=1)
                    parts.append(dots[half * blk:(half + 1) * blk, :] + line)
                value = jnp.exp2(jnp.concatenate(parts, axis=0))
                if 2 * k == reach:
                    value = jnp.where(row2 == col2, 0.0, value)
            else:
                value = jnp.exp2(dots - factor)
                rows_of = []
                for half in range(2):
                    cols_of = []
                    for j in range(2):
                        hub = hub_ref[2 * (k - reach - 1) + j]
                        off = (hub - (base_block + 2 * m + half)) * 1024
                        tile = value[half * blk:(half + 1) * blk, j * blk:(j + 1) * blk]
                        cols_of.append(jnp.where(row - col + off == 0, 0.0, tile))
                    rows_of.append(jnp.concatenate(cols_of, axis=1))
                value = jnp.concatenate(rows_of, axis=0)
            total = total + value[:, :blk] + value[:, blk:]
            weights[m, :, k * two:(k + 1) * two] = value.astype(jnp.bfloat16)
        degree = jnp.sum(total, axis=1, keepdims=True)
        inv_root[pl.ds(pl.multiple_of(m * two, two), two), :] = jnp.broadcast_to(
            lax.rsqrt(degree), (two, blk))
        return carry

    lax.fori_loop(0, pairs, weigh, 0)

    lane = lax.broadcasted_iota(jnp.int32, (two, quarter), 1)

    def wide(ref, m):
        value = ref[pl.ds(pl.multiple_of(m * two, two), two), :]
        return jnp.concatenate([value] * (quarter // blk), axis=1)

    def begin(m, carry):
        seeds = wide(label_col, m) == lane + q * quarter
        labels[0, pl.ds(pl.multiple_of(reach * blk + m * two, blk), two), :] = jnp.where(
            seeds, wide(inv_root, m), 0.0).astype(jnp.bfloat16)
        return carry

    lax.fori_loop(0, pairs, begin, 0)

    half_rows = reach * blk
    for t in range(ITERS):
        z_down = remote(labels.at[t, low:low + half_rows], labels.at[t, high:high + half_rows],
                        z_send.at[t, 0], z_recv.at[t, 0], down)
        z_up = remote(labels.at[t, high - half_rows:high], labels.at[t, 0:half_rows],
                      z_send.at[t, 1], z_recv.at[t, 1], up)
        held = jnp.dot(pick[...], labels[t, low:high, :],
                       preferred_element_type=jnp.float32).astype(jnp.bfloat16)
        for s in range(stages):
            lab_send[t, s] = held
            copy = remote(lab_send.at[t, s], lab_recv.at[t, s],
                          l_send.at[t, s], l_recv.at[t, s], partners[s])
            copy.start()
            if s == 0:
                z_down.start()
                z_up.start()
            pending.append(copy)
            copy.wait_recv()
            held = held + lab_recv[t, s]
        labels[t, window * blk:(window + hubs) * blk, :] = held
        z_down.wait_recv()
        z_up.wait_recv()
        pending += [z_down, z_up]

        def apply(m, carry):
            total = jnp.dot(weights[m, :, :span],
                            labels[t, pl.ds(pl.multiple_of(m * two, two), span), :],
                            preferred_element_type=jnp.float32)
            total = total + jnp.dot(weights[m, :, span:],
                                    labels[t, window * blk:(window + hubs) * blk, :],
                                    preferred_element_type=jnp.float32)
            root = wide(inv_root, m)
            spread = spread_rate * root * total
            if t < ITERS - 1:
                seeds = wide(label_col, m) == lane + q * quarter
                spread = spread + jnp.where(seeds, 1.0 - spread_rate, 0.0)
                labels[t + 1, pl.ds(pl.multiple_of(reach * blk + m * two, blk), two), :] = (
                    root * spread).astype(jnp.bfloat16)
            else:
                rows = pl.ds(pl.multiple_of(m * two, two), two)
                res[rows, :] = spread
                res_half[rows, :] = spread.astype(jnp.bfloat16)
            return carry

        lax.fori_loop(0, pairs, apply, 0)

    own_rows = own_blocks * blk

    def rows_of(index):
        return pl.ds(pl.multiple_of(index * own_rows, blk), own_rows)

    last = [
        remote(res_half.at[rows_of(q_x)], from_x, r_send.at[1], r_recv.at[1], xp),
        remote(res_half.at[rows_of(q_d)], from_d, r_send.at[2], r_recv.at[2], dp),
        remote(res.at[rows_of(q_sib)], from_sib, r_send.at[0], r_recv.at[0], sib),
    ]
    for copy in last:
        copy.start()
    for copy in last:
        copy.wait_recv()
    pending += last

    lane1 = lax.broadcasted_iota(jnp.int32, (blk, quarter), 1)
    for n in range(own_blocks):
        rows = pl.ds(n * blk, blk)
        group_rows = pl.ds(pl.multiple_of(q * own_rows + n * blk, blk), blk)
        label = label_col[group_rows, :]
        label = jnp.concatenate([label] * (quarter // blk), axis=1)
        pieces = [(q, res[group_rows, :]), (q_sib, from_sib[rows, :]),
                  (q_x, from_x[rows, :].astype(jnp.float32)),
                  (q_d, from_d[rows, :].astype(jnp.float32))]
        values = []
        total = jnp.zeros((blk, 1), jnp.float32)
        for index, piece in pieces:
            seeds = label == lane1 + index * quarter
            value = piece + jnp.where(seeds, 1.0 - spread_rate, 0.0)
            total = total + jnp.sum(value, axis=1, keepdims=True)
            values.append((index, value))
        scale = cols / total
        for index, value in values:
            out_ref[rows, pl.ds(pl.multiple_of(index * quarter, quarter), quarter)] = jnp.log(
                1.0 + value * scale)
    for copy in pending:
        copy.wait_send()


def on_device(cols, features, seed_labels, neighbours, hub_blocks):
    device = lax.axis_index("rows")
    devices = lax.axis_size("rows")
    own_blocks, slots = neighbours.shape
    rows, width = features.shape
    blk = rows // own_blocks
    all_blocks = devices * own_blocks
    reach = 2 * own_blocks
    groups = devices // GROUP
    stages = groups.bit_length() - 1
    group_blocks = GROUP * own_blocks
    table_rows = (group_blocks + 2 * reach + GROUP) * blk
    pairs = group_blocks // 2
    span = (2 * reach + 2 + GROUP) * blk
    quarter = cols // GROUP

    ids = device * own_blocks + jnp.arange(own_blocks, dtype=jnp.int32)
    parity = ids % 2
    position = (neighbours - ids[:, None] + reach + all_blocks) % all_blocks + parity[:, None]
    count = jnp.sum(
        (position[:, :, None] == jnp.arange(128, dtype=jnp.int32)[None, None, :]), axis=1
    ).astype(jnp.float32)
    bias = jnp.where(count > 0, jnp.log2(jnp.maximum(count, 1.0)) - LOG2E / kernel_width, -1e4)
    lines = seed_labels.reshape(own_blocks, blk).astype(jnp.float32)
    pad = ((0, 8 - own_blocks), (0, 0))
    meta = jnp.concatenate([jnp.pad(lines, pad), jnp.pad(bias, pad)], axis=0)

    vmem = pl.BlockSpec(memory_space=pltpu.VMEM)
    dma = pltpu.SemaphoreType.DMA
    return pl.pallas_call(
        functools.partial(kernel, groups, blk, cols),
        out_shape=jax.ShapeDtypeStruct((rows, cols), jnp.float32),
        in_specs=[vmem, vmem, pl.BlockSpec(memory_space=pltpu.SMEM)],
        out_specs=vmem,
        scratch_shapes=[
            pltpu.VMEM((table_rows, width), jnp.bfloat16),
            pltpu.VMEM((pairs, 2 * blk, span), jnp.bfloat16),
            pltpu.VMEM((ITERS, table_rows, quarter), jnp.bfloat16),
            pltpu.VMEM((group_blocks * blk, blk), jnp.float32),
            pltpu.VMEM((group_blocks * blk, blk), jnp.int32),
            pltpu.VMEM((GROUP, 16, 128), jnp.float32),
            pltpu.VMEM((group_blocks + 4, 128), jnp.float32),
            pltpu.VMEM((stages, blk, width), jnp.bfloat16),
            pltpu.VMEM((stages, blk, width), jnp.bfloat16),
            pltpu.VMEM((ITERS, stages, GROUP * blk, quarter), jnp.bfloat16),
            pltpu.VMEM((ITERS, stages, GROUP * blk, quarter), jnp.bfloat16),
            pltpu.VMEM((group_blocks * blk, quarter), jnp.float32),
            pltpu.VMEM((group_blocks * blk, quarter), jnp.bfloat16),
            pltpu.VMEM((rows, quarter), jnp.float32),
            pltpu.VMEM((rows, quarter), jnp.bfloat16),
            pltpu.VMEM((rows, quarter), jnp.bfloat16),
            pltpu.VMEM((GROUP * blk, group_blocks * blk), jnp.bfloat16),
            dma((7, own_blocks)), dma((7, own_blocks)),
            dma((3,)), dma((3,)),
            dma((stages,)), dma((stages,)),
            dma((3,)), dma((3,)),
            dma((ITERS, 2)), dma((ITERS, 2)),
            dma((ITERS, stages)), dma((ITERS, stages)),
            dma((3,)), dma((3,)),
        ],
        compiler_params=pltpu.CompilerParams(
            collective_id=0, has_side_effects=True, vmem_limit_bytes=60 * 1024 * 1024),
    )(features, meta, hub_blocks)


def solution(mesh):
    placed = (
        P(("region", "rows"), None),
        P(("region", "rows")),
        P(("region", "rows"), None),
        P("region"),
    )
    return jax.shard_map(
        functools.partial(on_device, 1024),
        mesh=mesh,
        in_specs=placed,
        out_specs=P(("region", "rows"), None),
        check_vma=False,
    )
```

```python
import functools
import math

import jax
import jax.numpy as jnp
from jax import lax
from jax.experimental import pallas as pl
from jax.experimental.pallas import tpu as pltpu
from jax.sharding import PartitionSpec as P

ITERS = 3
GROUP = 4
LOG2E = math.log2(math.e)

spread_rate = 0.9
kernel_width = 0.25
epsilon = 1e-06


def kernel(groups, blk, cols, feat_ref, meta_ref, hub_ref, out_ref,
           table, weights, labels, inv_root, label_col, meta, bias,
           hub_bufs, small_bufs, lab_bufs, lines, res, res_half, from_sib, from_x, from_d, pick,
           f_send, f_recv, m_send, m_recv, p_send, p_recv, n_send, n_recv,
           c_send, c_recv, z_send, z_recv, r_send, r_recv):
    own_blocks = feat_ref.shape[0] // blk
    width = feat_ref.shape[1]
    reach = 2 * own_blocks
    group_blocks = GROUP * own_blocks
    window = group_blocks + 2 * reach
    hubs = GROUP
    pairs = group_blocks // 2
    span = (2 * reach + 2) * blk
    quarter = cols // GROUP

    me = lax.axis_index("rows")
    g, q = lax.div(me, GROUP), lax.rem(me, GROUP)
    c, x = lax.rem(q, 2), lax.div(q, 2)
    q_sib = q + 1 - 2 * c
    q_x = q + 2 - 4 * x
    q_d = q_x + 1 - 2 * c
    sib, xp, dp = g * GROUP + q_sib, g * GROUP + q_x, g * GROUP + q_d
    up = lax.rem(g + 1, groups) * GROUP + q
    down = lax.rem(g + groups - 1, groups) * GROUP + q
    first = x * up + (1 - x) * down
    second = x * down + (1 - x) * up
    def remote(src, dst, send, recv, device):
        return pltpu.make_async_remote_copy(
            src_ref=src, dst_ref=dst, send_sem=send, recv_sem=recv,
            device_id={"rows": device}, device_id_type=pl.DeviceIdType.MESH)

    barrier = pltpu.get_barrier_semaphore()
    everyone = [sib, xp, dp, up, down]
    for device in everyone:
        pl.semaphore_signal(barrier, inc=1, device_id={"rows": device},
                            device_id_type=pl.DeviceIdType.MESH)
    pl.semaphore_wait(barrier, len(everyone))

    pending = []
    ends = []

    def chain(held, bufs, index, between):
        to_up = remote(bufs.at[2], bufs.at[0], c_send.at[index, 0], c_recv.at[index, 0], up)
        to_down = remote(bufs.at[3], bufs.at[1], c_send.at[index, 1], c_recv.at[index, 1], down)
        ends.append((to_up, to_down))
        inner = jnp.logical_and(g > 0, g < groups - 1)

        @pl.when(g == 0)
        def _():
            bufs[0] = jnp.zeros_like(held)
            bufs[2] = held
            to_up.start()

        @pl.when(g == groups - 1)
        def _():
            bufs[1] = jnp.zeros_like(held)
            bufs[3] = held
            to_down.start()

        between()

        @pl.when(g > 0)
        def _():
            to_up.wait_recv()

        @pl.when(inner)
        def _():
            bufs[2] = held + bufs[0]
            to_up.start()

        @pl.when(g < groups - 1)
        def _():
            to_down.wait_recv()

        @pl.when(inner)
        def _():
            bufs[3] = held + bufs[1]
            to_down.start()

        return held + bufs[0] + bufs[1]

    def at(position):
        return pl.ds(pl.multiple_of(position * blk, blk), blk)

    meta[q] = meta_ref[...]
    meta_copies = []
    for k, device in enumerate((sib, xp, dp)):
        copy = remote(meta.at[q], meta.at[q], m_send.at[k], m_recv.at[k], device)
        copy.start()
        meta_copies.append(copy)

    pos_a = reach + own_blocks * q
    pos_b = reach + own_blocks * q_x
    edge = reach + group_blocks
    dst_a = x * (own_blocks * c) + (1 - x) * (edge + own_blocks * c)
    dst_b = (1 - x) * (own_blocks * c) + x * (edge + own_blocks * c)

    def fcopy(kind, n, src, dst, device):
        return remote(table.at[at(src + n)], table.at[at(dst + n)],
                      f_send.at[kind, n], f_recv.at[kind, n], device)

    a_x, a_z, a_s, b_z, b_s, ha_s, hb_s = [], [], [], [], [], [], []
    for n in range(own_blocks):
        values = feat_ref[n * blk:(n + 1) * blk, :].astype(jnp.float32)
        mean = jnp.sum(values * values, axis=1, keepdims=True) * (1.0 / width)
        scaled = values * lax.rsqrt(mean + epsilon)
        table[at(pos_a + n), :] = (scaled * width ** (-0.5)).astype(jnp.bfloat16)
        a_x.append(fcopy(0, n, pos_a, pos_a, xp))
        a_z.append(fcopy(1, n, pos_a, dst_a, first))
        a_s.append(fcopy(2, n, pos_a, pos_a, sib))
        a_x[n].start()
        a_z[n].start()
        a_s[n].start()
    for n in range(own_blocks):
        a_x[n].wait_recv()
        b_z.append(fcopy(3, n, pos_b, dst_b, second))
        b_s.append(fcopy(4, n, pos_b, pos_b, sib))
        b_z[n].start()
        b_s[n].start()
    for n in range(own_blocks):
        a_s[n].wait_recv()
        b_s[n].wait_recv()

    base_block = g * group_blocks
    row = lax.broadcasted_iota(jnp.int32, (blk, blk), 0)
    col = lax.broadcasted_iota(jnp.int32, (blk, blk), 1)
    for h in range(hubs):
        for n in range(group_blocks):
            off = (hub_ref[h] - (base_block + n)) * 1024
            pick[h * blk:(h + 1) * blk, n * blk:(n + 1) * blk] = jnp.where(
                row - col + off == 0, 1.0, 0.0).astype(jnp.bfloat16)
    low, high = reach * blk, (reach + group_blocks) * blk
    held = jnp.dot(pick[at(q), :], table[low:high, :],
                   preferred_element_type=jnp.float32).astype(jnp.bfloat16)
    for copy in meta_copies:
        copy.wait_recv()
    lines[0] = jnp.zeros_like(lines[0])
    for n in range(group_blocks):
        owner, at_n = n // own_blocks, n % own_blocks
        for p in range(reach * 2 + 2):
            bias[n:n + 1, p * blk:(p + 1) * blk] = jnp.broadcast_to(
                meta[owner, 8 + at_n:9 + at_n, p:p + 1], (1, blk))
        line = meta[owner, at_n:at_n + 1, :]
        lines[0, 24 + n:25 + n, :] = line
        line = jnp.broadcast_to(line, (blk, blk))
        column = jnp.sum(jnp.where(row == col, line, 0.0), axis=1, keepdims=True)
        label_col[n * blk:(n + 1) * blk, :] = jnp.broadcast_to(column, (blk, blk)).astype(jnp.int32)

    two = 2 * blk
    row2 = lax.broadcasted_iota(jnp.int32, (two, two), 0)
    col2 = lax.broadcasted_iota(jnp.int32, (two, two), 1)
    factor = LOG2E / kernel_width
    chunks = reach + 1

    def step(value, unit):
        return value * unit if isinstance(value, int) else pl.multiple_of(value * unit, unit)

    def add_degree(m, value):
        rows = pl.ds(step(m, two), two)
        inv_root[rows, :] += value[:, :blk] + value[:, blk:]

    def chunk(m, k):
        own = table[pl.ds(step(m, two) + reach * blk, two), :]
        slab = table[pl.ds(step(m + k, two), two), :]
        dots = lax.dot_general(own, slab, (((1,), (1,)), ((), ())),
                               preferred_element_type=jnp.float32)
        there = pl.ds(step(k, two), two)
        value = jnp.exp2(jnp.concatenate(
            [dots[:blk, :] * factor + bias[pl.ds(2 * m, 1), there],
             dots[blk:, :] * factor + bias[pl.ds(2 * m + 1, 1), there]], axis=0))
        if not isinstance(k, int):
            value = jnp.where(row2 - col2 + (2 * k - reach) * 1024 == 0, 0.0, value)
        elif 2 * k == reach:
            value = jnp.where(row2 == col2, 0.0, value)
        add_degree(m, value)
        weights[m, :, there] = value.astype(jnp.bfloat16)

    inv_root[...] = jnp.zeros_like(inv_root)
    half = reach // 2

    def inside(m):
        lowest = max(half - m, 0) if isinstance(m, int) else jnp.maximum(half - m, 0)
        highest = (min(half + pairs - 1 - m, reach) if isinstance(m, int)
                   else jnp.minimum(half + pairs - 1 - m, reach))
        return lowest, (highest - lowest + 1) // 2 if isinstance(m, int) else lax.div(
            highest - lowest + 1, 2)

    def weigh_inside(m, carry):
        lowest, count = inside(m)

        def body(i, carry):
            chunk(m, lowest + 2 * i)
            chunk(m, lowest + 2 * i + 1)
            return carry

        return lax.fori_loop(0, count, body, carry)

    held = chain(held, hub_bufs, 0, lambda: lax.fori_loop(0, pairs // 2, weigh_inside, 0))
    table[at(window + q), :] = held
    hub_copies = []
    for k, device in enumerate((sib, xp, dp)):
        copy = remote(table.at[at(window + q)], table.at[at(window + q)],
                      p_send.at[k], p_recv.at[k], device)
        copy.start()
        hub_copies.append(copy)
    lax.fori_loop(pairs // 2, pairs, weigh_inside, 0)

    for n in range(own_blocks):
        a_z[n].wait_recv()
        ha_s.append(fcopy(5, n, dst_a, dst_a, sib))
        ha_s[n].start()
    for n in range(own_blocks):
        b_z[n].wait_recv()
        hb_s.append(fcopy(6, n, dst_b, dst_b, sib))
        hb_s[n].start()

    for copy in ha_s + hb_s + hub_copies:
        copy.wait_recv()
    pending += meta_copies + a_x + a_z + a_s + b_z + b_s + ha_s + hb_s + hub_copies

    for m in range(pairs):
        lowest, count = inside(m)
        for k in range(chunks):
            if not lowest <= k < lowest + 2 * count:
                chunk(m, k)

    def weigh_hubs(m, carry):
        own = table[pl.ds(step(m, two) + reach * blk, two), :]
        total = jnp.zeros((two, blk), jnp.float32)
        for k in range(hubs // 2):
            slab = table[pl.ds(window * blk + k * two, two), :]
            dots = lax.dot_general(own, slab, (((1,), (1,)), ((), ())),
                                   preferred_element_type=jnp.float32)
            value = jnp.exp2(dots * factor - factor)
            rows_of = []
            for part in range(2):
                cols_of = []
                for j in range(2):
                    off = (hub_ref[2 * k + j] - (base_block + 2 * m + part)) * 1024
                    tile = value[part * blk:(part + 1) * blk, j * blk:(j + 1) * blk]
                    cols_of.append(jnp.where(row - col + off == 0, 0.0, tile))
                rows_of.append(jnp.concatenate(cols_of, axis=1))
            value = jnp.concatenate(rows_of, axis=0)
            total = total + value[:, :blk] + value[:, blk:]
            weights[m, :, span + k * two:span + (k + 1) * two] = value.astype(jnp.bfloat16)
        rows = pl.ds(step(m, two), two)
        degree = jnp.sum(inv_root[rows, :] + total, axis=1, keepdims=True)
        inv_root[rows, :] = jnp.broadcast_to(lax.rsqrt(degree), (two, blk))
        return carry

    lax.fori_loop(0, pairs, weigh_hubs, 0)

    lane = lax.broadcasted_iota(jnp.int32, (two, quarter), 1)
    lane1 = lax.broadcasted_iota(jnp.int32, (blk, quarter), 1)

    def wide(ref, m):
        value = ref[pl.ds(step(m, two), two), :]
        return jnp.concatenate([value] * (quarter // blk), axis=1)

    for n in range(group_blocks):
        lines[0, n:n + 1, :] = jnp.sum(
            jnp.where(row == col, inv_root[n * blk:(n + 1) * blk, :], 0.0), axis=0, keepdims=True)
    n_up = remote(lines.at[0], lines.at[1], n_send.at[0], n_recv.at[0], up)
    n_down = remote(lines.at[0], lines.at[2], n_send.at[1], n_recv.at[1], down)
    pending += [n_up, n_down]
    block_row = lax.broadcasted_iota(jnp.int32, (group_blocks, blk), 0) + base_block
    found = []
    for start in (0, 24):
        for h in range(hubs):
            found.append(jnp.sum(jnp.where(block_row - hub_ref[h] == 0,
                                           lines[0, start:start + group_blocks, :], 0.0),
                                 axis=0, keepdims=True))
    low_block = reach + group_blocks

    def begin(m, carry):
        seeds = wide(label_col, m) == lane + q * quarter
        labels[0, pl.ds(step(m, two) + reach * blk, two), :] = jnp.where(
            seeds, wide(inv_root, m), 0.0).astype(jnp.bfloat16)
        return carry

    def between_small():
        n_up.start()
        n_down.start()
        lax.fori_loop(0, pairs, begin, 0)

    small = chain(jnp.concatenate(found, axis=0), small_bufs, 1, between_small)
    n_up.wait_recv()
    n_down.wait_recv()

    def first_labels(position, root, label):
        def column(line):
            return jnp.sum(jnp.where(row == col, jnp.broadcast_to(line, (blk, blk)), 0.0),
                           axis=1, keepdims=True)
        seeds = column(label).astype(jnp.int32) == lane1 + q * quarter
        labels[0, position * blk:(position + 1) * blk, :] = jnp.where(
            seeds, column(root), 0.0).astype(jnp.bfloat16)

    for n in range(reach):
        at_n = group_blocks - reach + n
        first_labels(n, lines[1, at_n:at_n + 1, :], lines[1, 24 + at_n:25 + at_n, :])
        first_labels(low_block + n, lines[2, n:n + 1, :], lines[2, 24 + n:25 + n, :])
    for h in range(hubs):
        first_labels(window + h, small[h:h + 1, :], small[hubs + h:hubs + h + 1, :])

    half_rows = reach * blk
    for t in range(ITERS):
        if t > 0:
            z_down = remote(labels.at[t, low:low + half_rows], labels.at[t, high:high + half_rows],
                            z_send.at[t - 1, 0], z_recv.at[t - 1, 0], down)
            z_up = remote(labels.at[t, high - half_rows:high], labels.at[t, 0:half_rows],
                          z_send.at[t - 1, 1], z_recv.at[t - 1, 1], up)
            held = jnp.dot(pick[...], labels[t, low:high, :],
                           preferred_element_type=jnp.float32).astype(jnp.bfloat16)

            def start_halo():
                z_down.start()
                z_up.start()

            labels[t, window * blk:(window + hubs) * blk, :] = chain(
                held, lab_bufs.at[t - 1], 1 + t, start_halo)
            z_down.wait_recv()
            z_up.wait_recv()
            pending += [z_down, z_up]

        def apply(m, carry):
            total = jnp.dot(weights[m, :, :span],
                            labels[t, pl.ds(pl.multiple_of(m * two, two), span), :],
                            preferred_element_type=jnp.float32)
            total = total + jnp.dot(weights[m, :, span:],
                                    labels[t, window * blk:(window + hubs) * blk, :],
                                    preferred_element_type=jnp.float32)
            root = wide(inv_root, m)
            spread = spread_rate * root * total
            if t < ITERS - 1:
                seeds = wide(label_col, m) == lane + q * quarter
                spread = spread + jnp.where(seeds, 1.0 - spread_rate, 0.0)
                labels[t + 1, pl.ds(pl.multiple_of(reach * blk + m * two, blk), two), :] = (
                    root * spread).astype(jnp.bfloat16)
            else:
                rows = pl.ds(pl.multiple_of(m * two, two), two)
                res[rows, :] = spread
                res_half[rows, :] = spread.astype(jnp.bfloat16)
            return carry

        if t < ITERS - 1:
            lax.fori_loop(0, pairs, apply, 0)

    own_rows = own_blocks * blk

    def rows_of(index):
        return pl.ds(pl.multiple_of(index * own_rows, blk), own_rows)

    last = [
        remote(res_half.at[rows_of(q_x)], from_x, r_send.at[1], r_recv.at[1], xp),
        remote(res_half.at[rows_of(q_d)], from_d, r_send.at[2], r_recv.at[2], dp),
        remote(res.at[rows_of(q_sib)], from_sib, r_send.at[0], r_recv.at[0], sib),
    ]
    there = (1 - x) * (pairs // 2)
    lax.fori_loop(0, pairs // 2, lambda m, carry: apply(there + m, carry), 0)
    last[0].start()
    last[1].start()
    here = x * (pairs // 2)
    lax.fori_loop(0, pairs // 2, lambda m, carry: apply(here + m, carry), 0)
    last[2].start()
    for copy in last:
        copy.wait_recv()
    pending += last

    for n in range(own_blocks):
        rows = pl.ds(n * blk, blk)
        group_rows = pl.ds(pl.multiple_of(q * own_rows + n * blk, blk), blk)
        label = label_col[group_rows, :]
        label = jnp.concatenate([label] * (quarter // blk), axis=1)
        pieces = [(q, res[group_rows, :]), (q_sib, from_sib[rows, :]),
                  (q_x, from_x[rows, :].astype(jnp.float32)),
                  (q_d, from_d[rows, :].astype(jnp.float32))]
        values = []
        total = jnp.zeros((blk, 1), jnp.float32)
        for index, piece in pieces:
            seeds = label == lane1 + index * quarter
            value = piece + jnp.where(seeds, 1.0 - spread_rate, 0.0)
            total = total + jnp.sum(value, axis=1, keepdims=True)
            values.append((index, value))
        scale = cols / total
        for index, value in values:
            out_ref[rows, pl.ds(pl.multiple_of(index * quarter, quarter), quarter)] = jnp.log(
                1.0 + value * scale)
    for copy in pending:
        copy.wait_send()
    for to_up, to_down in ends:
        @pl.when(g < groups - 1)
        def _():
            to_up.wait_send()

        @pl.when(g > 0)
        def _():
            to_down.wait_send()


def on_device(cols, features, seed_labels, neighbours, hub_blocks):
    device = lax.axis_index("rows")
    devices = lax.axis_size("rows")
    own_blocks, slots = neighbours.shape
    rows, width = features.shape
    blk = rows // own_blocks
    all_blocks = devices * own_blocks
    reach = 2 * own_blocks
    groups = devices // GROUP
    group_blocks = GROUP * own_blocks
    table_rows = (group_blocks + 2 * reach + GROUP) * blk
    pairs = group_blocks // 2
    span = (2 * reach + 2 + GROUP) * blk
    quarter = cols // GROUP

    ids = device * own_blocks + jnp.arange(own_blocks, dtype=jnp.int32)
    parity = ids % 2
    position = (neighbours - ids[:, None] + reach + all_blocks) % all_blocks + parity[:, None]
    count = jnp.sum(
        (position[:, :, None] == jnp.arange(128, dtype=jnp.int32)[None, None, :]), axis=1
    ).astype(jnp.float32)
    bias = jnp.where(count > 0, jnp.log2(jnp.maximum(count, 1.0)) - LOG2E / kernel_width, -1e4)
    lines = seed_labels.reshape(own_blocks, blk).astype(jnp.float32)
    pad = ((0, 8 - own_blocks), (0, 0))
    meta = jnp.concatenate([jnp.pad(lines, pad), jnp.pad(bias, pad)], axis=0)

    vmem = pl.BlockSpec(memory_space=pltpu.VMEM)
    dma = pltpu.SemaphoreType.DMA
    return pl.pallas_call(
        functools.partial(kernel, groups, blk, cols),
        out_shape=jax.ShapeDtypeStruct((rows, cols), jnp.float32),
        in_specs=[vmem, vmem, pl.BlockSpec(memory_space=pltpu.SMEM)],
        out_specs=vmem,
        scratch_shapes=[
            pltpu.VMEM((table_rows, width), jnp.bfloat16),
            pltpu.VMEM((pairs, 2 * blk, span), jnp.bfloat16),
            pltpu.VMEM((ITERS, table_rows, quarter), jnp.bfloat16),
            pltpu.VMEM((group_blocks * blk, blk), jnp.float32),
            pltpu.VMEM((group_blocks * blk, blk), jnp.int32),
            pltpu.VMEM((GROUP, 16, 128), jnp.float32),
            pltpu.VMEM((group_blocks, (2 * reach + 2) * blk), jnp.float32),
            pltpu.VMEM((4, blk, width), jnp.bfloat16),
            pltpu.VMEM((4, 2 * GROUP, 128), jnp.float32),
            pltpu.VMEM((ITERS - 1, 4, GROUP * blk, quarter), jnp.bfloat16),
            pltpu.VMEM((3, 48, 128), jnp.float32),
            pltpu.VMEM((group_blocks * blk, quarter), jnp.float32),
            pltpu.VMEM((group_blocks * blk, quarter), jnp.bfloat16),
            pltpu.VMEM((rows, quarter), jnp.float32),
            pltpu.VMEM((rows, quarter), jnp.bfloat16),
            pltpu.VMEM((rows, quarter), jnp.bfloat16),
            pltpu.VMEM((GROUP * blk, group_blocks * blk), jnp.bfloat16),
            dma((7, own_blocks)), dma((7, own_blocks)),
            dma((3,)), dma((3,)),
            dma((3,)), dma((3,)),
            dma((2,)), dma((2,)),
            dma((ITERS + 1, 2)), dma((ITERS + 1, 2)),
            dma((ITERS - 1, 2)), dma((ITERS - 1, 2)),
            dma((3,)), dma((3,)),
        ],
        compiler_params=pltpu.CompilerParams(
            collective_id=0, has_side_effects=True, vmem_limit_bytes=60 * 1024 * 1024),
    )(features, meta, hub_blocks)


def solution(mesh):
    placed = (
        P(("region", "rows"), None),
        P(("region", "rows")),
        P(("region", "rows"), None),
        P("region"),
    )
    return jax.shard_map(
        functools.partial(on_device, 1024),
        mesh=mesh,
        in_specs=placed,
        out_specs=P(("region", "rows"), None),
        check_vma=False,
    )
```

```python
import functools
import math

import jax
import jax.numpy as jnp
from jax import lax
from jax.experimental import pallas as pl
from jax.experimental.pallas import tpu as pltpu
from jax.sharding import PartitionSpec as P

ITERS = 3
GROUP = 4
LOG2E = math.log2(math.e)

spread_rate = 0.9
kernel_width = 0.25
epsilon = 1e-06


def kernel(groups, blk, cols, feat_ref, meta_ref, hub_ref, out_ref,
           table, weights, labels, inv_root, label_col, meta, bias,
           hub_bufs, small_bufs, lab_bufs, lines, res, res_half, from_sib, from_x, from_d, pick,
           f_send, f_recv, m_send, m_recv, p_send, p_recv, n_send, n_recv,
           c_send, c_recv, z_send, z_recv, r_send, r_recv):
    own_blocks = feat_ref.shape[0] // blk
    width = feat_ref.shape[1]
    reach = 2 * own_blocks
    group_blocks = GROUP * own_blocks
    window = group_blocks + 2 * reach
    hubs = GROUP
    pairs = group_blocks // 2
    span = (2 * reach + 2) * blk
    quarter = cols // GROUP

    me = lax.axis_index("rows")
    g, q = lax.div(me, GROUP), lax.rem(me, GROUP)
    c, x = lax.rem(q, 2), lax.div(q, 2)
    q_sib = q + 1 - 2 * c
    q_x = q + 2 - 4 * x
    q_d = q_x + 1 - 2 * c
    sib, xp, dp = g * GROUP + q_sib, g * GROUP + q_x, g * GROUP + q_d
    up = lax.rem(g + 1, groups) * GROUP + q
    down = lax.rem(g + groups - 1, groups) * GROUP + q
    first = x * up + (1 - x) * down
    second = x * down + (1 - x) * up
    def remote(src, dst, send, recv, device):
        return pltpu.make_async_remote_copy(
            src_ref=src, dst_ref=dst, send_sem=send, recv_sem=recv,
            device_id={"rows": device}, device_id_type=pl.DeviceIdType.MESH)

    barrier = pltpu.get_barrier_semaphore()
    everyone = [sib, xp, dp, up, down]
    for device in everyone:
        pl.semaphore_signal(barrier, inc=1, device_id={"rows": device},
                            device_id_type=pl.DeviceIdType.MESH)
    pl.semaphore_wait(barrier, len(everyone))

    pending = []
    ends = []

    def chain(held, bufs, index, between, parts):
        count = held.shape[0] // parts
        rows = [slice(n * count, (n + 1) * count) for n in range(parts)]
        to_up = [remote(bufs.at[2, r], bufs.at[0, r], c_send.at[index, 0, n],
                        c_recv.at[index, 0, n], up) for n, r in enumerate(rows)]
        to_down = [remote(bufs.at[3, r], bufs.at[1, r], c_send.at[index, 1, n],
                          c_recv.at[index, 1, n], down) for n, r in enumerate(rows)]
        ends.append((to_up, to_down))
        inner = jnp.logical_and(g > 0, g < groups - 1)

        @pl.when(g == 0)
        def _():
            bufs[0] = jnp.zeros_like(held)
            bufs[2] = held
            for copy in to_up:
                copy.start()

        @pl.when(g == groups - 1)
        def _():
            bufs[1] = jnp.zeros_like(held)
            bufs[3] = held
            for copy in to_down:
                copy.start()

        between()

        for n, r in enumerate(rows):
            @pl.when(g > 0)
            def _():
                to_up[n].wait_recv()

            @pl.when(inner)
            def _():
                bufs[2, r, :] = held[r, :] + bufs[0, r, :]
                to_up[n].start()

            @pl.when(g < groups - 1)
            def _():
                to_down[n].wait_recv()

            @pl.when(inner)
            def _():
                bufs[3, r, :] = held[r, :] + bufs[1, r, :]
                to_down[n].start()

        return held + bufs[0] + bufs[1]

    def at(position):
        return pl.ds(pl.multiple_of(position * blk, blk), blk)

    meta[q] = meta_ref[...]
    meta_copies = []
    for k, device in enumerate((sib, xp, dp)):
        copy = remote(meta.at[q], meta.at[q], m_send.at[k], m_recv.at[k], device)
        copy.start()
        meta_copies.append(copy)

    pos_a = reach + own_blocks * q
    pos_b = reach + own_blocks * q_x
    edge = reach + group_blocks
    dst_a = x * (own_blocks * c) + (1 - x) * (edge + own_blocks * c)
    dst_b = (1 - x) * (own_blocks * c) + x * (edge + own_blocks * c)

    def fcopy(kind, n, src, dst, device):
        return remote(table.at[at(src + n)], table.at[at(dst + n)],
                      f_send.at[kind, n], f_recv.at[kind, n], device)

    a_x, a_z, a_s, b_z, b_s, ha_s, hb_s = [], [], [], [], [], [], []
    for n in range(own_blocks):
        values = feat_ref[n * blk:(n + 1) * blk, :].astype(jnp.float32)
        mean = jnp.sum(values * values, axis=1, keepdims=True) * (1.0 / width)
        scaled = values * lax.rsqrt(mean + epsilon)
        table[at(pos_a + n), :] = (scaled * width ** (-0.5)).astype(jnp.bfloat16)
        a_x.append(fcopy(0, n, pos_a, pos_a, xp))
        a_z.append(fcopy(1, n, pos_a, dst_a, first))
        a_s.append(fcopy(2, n, pos_a, pos_a, sib))
        a_x[n].start()
        a_z[n].start()
        a_s[n].start()
    for n in range(own_blocks):
        a_x[n].wait_recv()
        b_z.append(fcopy(3, n, pos_b, dst_b, second))
        b_s.append(fcopy(4, n, pos_b, pos_b, sib))
        b_z[n].start()
        b_s[n].start()
    for n in range(own_blocks):
        a_s[n].wait_recv()
        b_s[n].wait_recv()

    base_block = g * group_blocks
    row = lax.broadcasted_iota(jnp.int32, (blk, blk), 0)
    col = lax.broadcasted_iota(jnp.int32, (blk, blk), 1)
    for h in range(hubs):
        for n in range(group_blocks):
            off = (hub_ref[h] - (base_block + n)) * 1024
            pick[h * blk:(h + 1) * blk, n * blk:(n + 1) * blk] = jnp.where(
                row - col + off == 0, 1.0, 0.0).astype(jnp.bfloat16)
    low, high = reach * blk, (reach + group_blocks) * blk
    held = jnp.dot(pick[at(q), :], table[low:high, :],
                   preferred_element_type=jnp.float32).astype(jnp.bfloat16)
    for copy in meta_copies:
        copy.wait_recv()
    lines[0] = jnp.zeros_like(lines[0])
    for n in range(group_blocks):
        owner, at_n = n // own_blocks, n % own_blocks
        for p in range(reach * 2 + 2):
            bias[n:n + 1, p * blk:(p + 1) * blk] = jnp.broadcast_to(
                meta[owner, 8 + at_n:9 + at_n, p:p + 1], (1, blk))
        line = meta[owner, at_n:at_n + 1, :]
        lines[0, 24 + n:25 + n, :] = line
        line = jnp.broadcast_to(line, (blk, blk))
        column = jnp.sum(jnp.where(row == col, line, 0.0), axis=1, keepdims=True)
        label_col[n * blk:(n + 1) * blk, :] = jnp.broadcast_to(column, (blk, blk)).astype(jnp.int32)

    two = 2 * blk
    row2 = lax.broadcasted_iota(jnp.int32, (two, two), 0)
    col2 = lax.broadcasted_iota(jnp.int32, (two, two), 1)
    factor = LOG2E / kernel_width
    chunks = reach + 1

    def step(value, unit):
        return value * unit if isinstance(value, int) else pl.multiple_of(value * unit, unit)

    def add_degree(m, value):
        rows = pl.ds(step(m, two), two)
        inv_root[rows, :] += value[:, :blk] + value[:, blk:]

    def chunk(m, k):
        own = table[pl.ds(step(m, two) + reach * blk, two), :]
        slab = table[pl.ds(step(m + k, two), two), :]
        dots = lax.dot_general(own, slab, (((1,), (1,)), ((), ())),
                               preferred_element_type=jnp.float32)
        there = pl.ds(step(k, two), two)
        value = jnp.exp2(jnp.concatenate(
            [dots[:blk, :] * factor + bias[pl.ds(2 * m, 1), there],
             dots[blk:, :] * factor + bias[pl.ds(2 * m + 1, 1), there]], axis=0))
        if not isinstance(k, int):
            value = jnp.where(row2 - col2 + (2 * k - reach) * 1024 == 0, 0.0, value)
        elif 2 * k == reach:
            value = jnp.where(row2 == col2, 0.0, value)
        add_degree(m, value)
        weights[m, :, there] = value.astype(jnp.bfloat16)

    inv_root[...] = jnp.zeros_like(inv_root)
    half = reach // 2

    def inside(m):
        lowest = max(half - m, 0) if isinstance(m, int) else jnp.maximum(half - m, 0)
        highest = (min(half + pairs - 1 - m, reach) if isinstance(m, int)
                   else jnp.minimum(half + pairs - 1 - m, reach))
        return lowest, (highest - lowest + 1) // 2 if isinstance(m, int) else lax.div(
            highest - lowest + 1, 2)

    def weigh_inside(m, carry):
        lowest, count = inside(m)

        def body(i, carry):
            chunk(m, lowest + 2 * i)
            chunk(m, lowest + 2 * i + 1)
            return carry

        return lax.fori_loop(0, count, body, carry)

    held = chain(held, hub_bufs, 0, lambda: lax.fori_loop(0, pairs // 2, weigh_inside, 0), 4)
    table[at(window + q), :] = held
    hub_copies = []
    for k, device in enumerate((sib, xp, dp)):
        copy = remote(table.at[at(window + q)], table.at[at(window + q)],
                      p_send.at[k], p_recv.at[k], device)
        copy.start()
        hub_copies.append(copy)
    lax.fori_loop(pairs // 2, pairs, weigh_inside, 0)

    for n in range(own_blocks):
        a_z[n].wait_recv()
        ha_s.append(fcopy(5, n, dst_a, dst_a, sib))
        ha_s[n].start()
    for n in range(own_blocks):
        b_z[n].wait_recv()
        hb_s.append(fcopy(6, n, dst_b, dst_b, sib))
        hb_s[n].start()

    for copy in ha_s + hb_s + hub_copies:
        copy.wait_recv()
    pending += meta_copies + a_x + a_z + a_s + b_z + b_s + ha_s + hb_s + hub_copies

    for m in range(pairs):
        lowest, count = inside(m)
        for k in range(chunks):
            if not lowest <= k < lowest + 2 * count:
                chunk(m, k)

    def weigh_hubs(m, carry):
        own = table[pl.ds(step(m, two) + reach * blk, two), :]
        total = jnp.zeros((two, blk), jnp.float32)
        for k in range(hubs // 2):
            slab = table[pl.ds(window * blk + k * two, two), :]
            dots = lax.dot_general(own, slab, (((1,), (1,)), ((), ())),
                                   preferred_element_type=jnp.float32)
            value = jnp.exp2(dots * factor - factor)
            rows_of = []
            for part in range(2):
                cols_of = []
                for j in range(2):
                    off = (hub_ref[2 * k + j] - (base_block + 2 * m + part)) * 1024
                    tile = value[part * blk:(part + 1) * blk, j * blk:(j + 1) * blk]
                    cols_of.append(jnp.where(row - col + off == 0, 0.0, tile))
                rows_of.append(jnp.concatenate(cols_of, axis=1))
            value = jnp.concatenate(rows_of, axis=0)
            total = total + value[:, :blk] + value[:, blk:]
            weights[m, :, span + k * two:span + (k + 1) * two] = value.astype(jnp.bfloat16)
        rows = pl.ds(step(m, two), two)
        degree = jnp.sum(inv_root[rows, :] + total, axis=1, keepdims=True)
        inv_root[rows, :] = jnp.broadcast_to(lax.rsqrt(degree), (two, blk))
        return carry

    lax.fori_loop(0, pairs, weigh_hubs, 0)

    lane = lax.broadcasted_iota(jnp.int32, (two, quarter), 1)
    lane1 = lax.broadcasted_iota(jnp.int32, (blk, quarter), 1)

    def wide(ref, m):
        value = ref[pl.ds(step(m, two), two), :]
        return jnp.concatenate([value] * (quarter // blk), axis=1)

    for n in range(group_blocks):
        lines[0, n:n + 1, :] = jnp.sum(
            jnp.where(row == col, inv_root[n * blk:(n + 1) * blk, :], 0.0), axis=0, keepdims=True)
    n_up = remote(lines.at[0], lines.at[1], n_send.at[0], n_recv.at[0], up)
    n_down = remote(lines.at[0], lines.at[2], n_send.at[1], n_recv.at[1], down)
    pending += [n_up, n_down]
    block_row = lax.broadcasted_iota(jnp.int32, (group_blocks, blk), 0) + base_block
    found = []
    for start in (0, 24):
        for h in range(hubs):
            found.append(jnp.sum(jnp.where(block_row - hub_ref[h] == 0,
                                           lines[0, start:start + group_blocks, :], 0.0),
                                 axis=0, keepdims=True))
    low_block = reach + group_blocks

    def begin(m, carry):
        seeds = wide(label_col, m) == lane + q * quarter
        labels[0, pl.ds(step(m, two) + reach * blk, two), :] = jnp.where(
            seeds, wide(inv_root, m), 0.0).astype(jnp.bfloat16)
        return carry

    def between_small():
        n_up.start()
        n_down.start()
        lax.fori_loop(0, pairs, begin, 0)

    small = chain(jnp.concatenate(found, axis=0), small_bufs, 1, between_small, 1)
    n_up.wait_recv()
    n_down.wait_recv()

    def first_labels(position, root, label):
        def column(line):
            return jnp.sum(jnp.where(row == col, jnp.broadcast_to(line, (blk, blk)), 0.0),
                           axis=1, keepdims=True)
        seeds = column(label).astype(jnp.int32) == lane1 + q * quarter
        labels[0, position * blk:(position + 1) * blk, :] = jnp.where(
            seeds, column(root), 0.0).astype(jnp.bfloat16)

    for n in range(reach):
        at_n = group_blocks - reach + n
        first_labels(n, lines[1, at_n:at_n + 1, :], lines[1, 24 + at_n:25 + at_n, :])
        first_labels(low_block + n, lines[2, n:n + 1, :], lines[2, 24 + n:25 + n, :])
    for h in range(hubs):
        first_labels(window + h, small[h:h + 1, :], small[hubs + h:hubs + h + 1, :])

    half_rows = reach * blk
    for t in range(ITERS):
        if t > 0:
            halo = []
            for n in range(reach):
                at_n = n * blk
                halo.append(remote(labels.at[t, low + at_n:low + at_n + blk],
                                   labels.at[t, high + at_n:high + at_n + blk],
                                   z_send.at[t - 1, 0, n], z_recv.at[t - 1, 0, n], down))
                halo.append(remote(labels.at[t, high - half_rows + at_n:high - half_rows + at_n + blk],
                                   labels.at[t, at_n:at_n + blk],
                                   z_send.at[t - 1, 1, n], z_recv.at[t - 1, 1, n], up))
            held = jnp.dot(pick[...], labels[t, low:high, :],
                           preferred_element_type=jnp.float32).astype(jnp.bfloat16)

            def start_halo():
                for copy in halo:
                    copy.start()

            labels[t, window * blk:(window + hubs) * blk, :] = chain(
                held, lab_bufs.at[t - 1], 1 + t, start_halo, hubs)
            for copy in halo:
                copy.wait_recv()
            pending += halo

        def apply(m, carry):
            total = jnp.dot(weights[m, :, :span],
                            labels[t, pl.ds(pl.multiple_of(m * two, two), span), :],
                            preferred_element_type=jnp.float32)
            total = total + jnp.dot(weights[m, :, span:],
                                    labels[t, window * blk:(window + hubs) * blk, :],
                                    preferred_element_type=jnp.float32)
            root = wide(inv_root, m)
            spread = spread_rate * root * total
            if t < ITERS - 1:
                seeds = wide(label_col, m) == lane + q * quarter
                spread = spread + jnp.where(seeds, 1.0 - spread_rate, 0.0)
                labels[t + 1, pl.ds(pl.multiple_of(reach * blk + m * two, blk), two), :] = (
                    root * spread).astype(jnp.bfloat16)
            else:
                rows = pl.ds(pl.multiple_of(m * two, two), two)
                res[rows, :] = spread
                res_half[rows, :] = spread.astype(jnp.bfloat16)
            return carry

        if t < ITERS - 1:
            lax.fori_loop(0, pairs, apply, 0)

    own_rows = own_blocks * blk

    def result(kind, ref, index, target, device):
        return [remote(ref.at[pl.ds(pl.multiple_of(index * own_rows + n * blk, blk), blk)],
                       target.at[n * blk:(n + 1) * blk],
                       r_send.at[kind, n], r_recv.at[kind, n], device)
                for n in range(own_blocks)]

    across = result(1, res_half, q_x, from_x, xp) + result(2, res_half, q_d, from_d, dp)
    beside = result(0, res, q_sib, from_sib, sib)
    last = across + beside
    there = (1 - x) * (pairs // 2)
    lax.fori_loop(0, pairs // 2, lambda m, carry: apply(there + m, carry), 0)
    for copy in across:
        copy.start()
    here = x * (pairs // 2)
    lax.fori_loop(0, pairs // 2, lambda m, carry: apply(here + m, carry), 0)
    for copy in beside:
        copy.start()
    for copy in last:
        copy.wait_recv()
    pending += last

    for n in range(own_blocks):
        rows = pl.ds(n * blk, blk)
        group_rows = pl.ds(pl.multiple_of(q * own_rows + n * blk, blk), blk)
        label = label_col[group_rows, :]
        label = jnp.concatenate([label] * (quarter // blk), axis=1)
        pieces = [(q, res[group_rows, :]), (q_sib, from_sib[rows, :]),
                  (q_x, from_x[rows, :].astype(jnp.float32)),
                  (q_d, from_d[rows, :].astype(jnp.float32))]
        values = []
        total = jnp.zeros((blk, 1), jnp.float32)
        for index, piece in pieces:
            seeds = label == lane1 + index * quarter
            value = piece + jnp.where(seeds, 1.0 - spread_rate, 0.0)
            total = total + jnp.sum(value, axis=1, keepdims=True)
            values.append((index, value))
        scale = cols / total
        for index, value in values:
            out_ref[rows, pl.ds(pl.multiple_of(index * quarter, quarter), quarter)] = jnp.log(
                1.0 + value * scale)
    for copy in pending:
        copy.wait_send()
    for to_up, to_down in ends:
        @pl.when(g < groups - 1)
        def _():
            for copy in to_up:
                copy.wait_send()

        @pl.when(g > 0)
        def _():
            for copy in to_down:
                copy.wait_send()


def on_device(cols, features, seed_labels, neighbours, hub_blocks):
    device = lax.axis_index("rows")
    devices = lax.axis_size("rows")
    own_blocks, slots = neighbours.shape
    rows, width = features.shape
    blk = rows // own_blocks
    all_blocks = devices * own_blocks
    reach = 2 * own_blocks
    groups = devices // GROUP
    group_blocks = GROUP * own_blocks
    table_rows = (group_blocks + 2 * reach + GROUP) * blk
    pairs = group_blocks // 2
    span = (2 * reach + 2 + GROUP) * blk
    quarter = cols // GROUP

    ids = device * own_blocks + jnp.arange(own_blocks, dtype=jnp.int32)
    parity = ids % 2
    position = (neighbours - ids[:, None] + reach + all_blocks) % all_blocks + parity[:, None]
    count = jnp.sum(
        (position[:, :, None] == jnp.arange(128, dtype=jnp.int32)[None, None, :]), axis=1
    ).astype(jnp.float32)
    bias = jnp.where(count > 0, jnp.log2(jnp.maximum(count, 1.0)) - LOG2E / kernel_width, -1e4)
    lines = seed_labels.reshape(own_blocks, blk).astype(jnp.float32)
    pad = ((0, 8 - own_blocks), (0, 0))
    meta = jnp.concatenate([jnp.pad(lines, pad), jnp.pad(bias, pad)], axis=0)

    vmem = pl.BlockSpec(memory_space=pltpu.VMEM)
    dma = pltpu.SemaphoreType.DMA
    return pl.pallas_call(
        functools.partial(kernel, groups, blk, cols),
        out_shape=jax.ShapeDtypeStruct((rows, cols), jnp.float32),
        in_specs=[vmem, vmem, pl.BlockSpec(memory_space=pltpu.SMEM)],
        out_specs=vmem,
        scratch_shapes=[
            pltpu.VMEM((table_rows, width), jnp.bfloat16),
            pltpu.VMEM((pairs, 2 * blk, span), jnp.bfloat16),
            pltpu.VMEM((ITERS, table_rows, quarter), jnp.bfloat16),
            pltpu.VMEM((group_blocks * blk, blk), jnp.float32),
            pltpu.VMEM((group_blocks * blk, blk), jnp.int32),
            pltpu.VMEM((GROUP, 16, 128), jnp.float32),
            pltpu.VMEM((group_blocks, (2 * reach + 2) * blk), jnp.float32),
            pltpu.VMEM((4, blk, width), jnp.bfloat16),
            pltpu.VMEM((4, 2 * GROUP, 128), jnp.float32),
            pltpu.VMEM((ITERS - 1, 4, GROUP * blk, quarter), jnp.bfloat16),
            pltpu.VMEM((3, 48, 128), jnp.float32),
            pltpu.VMEM((group_blocks * blk, quarter), jnp.float32),
            pltpu.VMEM((group_blocks * blk, quarter), jnp.bfloat16),
            pltpu.VMEM((rows, quarter), jnp.float32),
            pltpu.VMEM((rows, quarter), jnp.bfloat16),
            pltpu.VMEM((rows, quarter), jnp.bfloat16),
            pltpu.VMEM((GROUP * blk, group_blocks * blk), jnp.bfloat16),
            dma((7, own_blocks)), dma((7, own_blocks)),
            dma((3,)), dma((3,)),
            dma((3,)), dma((3,)),
            dma((2,)), dma((2,)),
            dma((ITERS + 1, 2, GROUP)), dma((ITERS + 1, 2, GROUP)),
            dma((ITERS - 1, 2, reach)), dma((ITERS - 1, 2, reach)),
            dma((3, own_blocks)), dma((3, own_blocks)),
        ],
        compiler_params=pltpu.CompilerParams(
            collective_id=0, has_side_effects=True, vmem_limit_bytes=60 * 1024 * 1024),
    )(features, meta, hub_blocks)


def solution(mesh):
    placed = (
        P(("region", "rows"), None),
        P(("region", "rows")),
        P(("region", "rows"), None),
        P("region"),
    )
    return jax.shard_map(
        functools.partial(on_device, 1024),
        mesh=mesh,
        in_specs=placed,
        out_specs=P(("region", "rows"), None),
        check_vma=False,
    )
```
